256 devices in a mesh: dp: 8 (over z), col: 32 (over x, y, core).
Axes of the slice: x: 4, y: 4, z: 8, core: 2. Of those that a mesh axis runs over, the one named last changes fastest.
Arguments:
- gradient: bfloat16 [8, 4096, 14336], P('dp', None, 'col'), may hold values from -6 to 6
- carried_error: bfloat16 [8, 4096, 14336], P('dp', None, 'col'), may hold values from -4 to 4
- q_start: float32 [14336, 128], P('col'), may hold values from -6 to 6
Outputs:
- new_error: bfloat16 [8, 4096, 14336], P('dp', None, 'col')
- q_factor: float32 [14336, 128], P('col')
The draws below stay inside these ranges and needn't reach their ends.
All inputs are finite; a program needn't handle non-finite values.
Results may differ from the reference program's by a relative error of at most 0.0073.
Values may be sent and summed in bfloat16 or wider, within the bound.
No kernel may reach another device: no remote copies, remote signals or barrier semaphores. Data moves between devices by JAX's collectives and lax.ppermute only.
A program may use at most 64 MiB of HBM per device.

```python
import jax
import jax.numpy as jnp
from jax import lax

ROWS = 4096
RANK = 128
ITERS = 3
COLS = 14336
GROUPS = 8


def spiked(values, rng, source, target, shards_of, factor):
    owner, partner = [(jnp.arange(values.shape[dim]) // (values.shape[dim] // shards_of)).reshape([-1 if axis == dim else 1 for axis in range(values.ndim)]) for dim in (source, target)]
    chosen = jax.random.permutation(rng, shards_of)[partner]
    strong = (owner == chosen) | (owner == (partner + shards_of // 2) % shards_of)
    return jnp.where(strong, factor * values, values)


def level_of(stream_key, extent, split, smallest, high):
    level, own = 1.0, jax.random.fold_in(stream_key, 6)
    for position, shards_of in split:
        steps = jnp.exp(jax.random.uniform(jax.random.fold_in(own, position), (shards_of,), jnp.float32, smallest / len(split), high / len(split)))
        level = level * jnp.repeat(steps, extent[position] // shards_of).reshape([-1 if axis == position else 1 for axis in range(len(extent))])
    return level


def bell_draw(stream_key, shape, scale, most, pieces=(), held_as=jnp.bfloat16):
    values = scale * jax.random.normal(stream_key, shape, jnp.float32)
    if pieces:
        values = values * level_of(stream_key, shape, pieces, -0.22, 0.18)
    return jnp.clip(values, -most, most).astype(held_as)


def heavy_noise(stream_key, dims, width, bound, split, heavy, held_as=jnp.bfloat16):
    entries = width * jax.random.normal(stream_key, dims, jnp.float32)
    if split:
        entries = entries * level_of(stream_key, dims, split, -0.22, 0.18)
    return jnp.clip(spiked(entries, jax.random.fold_in(stream_key, 3), *heavy), -bound, bound).astype(held_as)


def setup_inputs(seed: int = 0) -> dict:
    splits = jax.random.split(jax.random.key(seed), 4)
    return {
        "gradient": heavy_noise(splits[0], (GROUPS, ROWS, COLS), 1.0, 6.0, ((0, 8), (2, 32)), (2, 1, 32, 2.75)),
        "carried_error": heavy_noise(splits[1], (GROUPS, ROWS, COLS), 0.5, 4.0, ((0, 8), (2, 32)), (0, 1, 8, 2.0)),
        "q_start": bell_draw(splits[2], (COLS, RANK), 1.0, 6.0, ((0, 32),), jnp.float32),
    }


def orthonormal(p_total):
    p_gram = jnp.dot(p_total.T, p_total, precision=lax.Precision.HIGHEST)
    factor_low = jnp.linalg.cholesky(p_gram)
    return lax.linalg.triangular_solve(factor_low, p_total, left_side=False, lower=True, transpose_a=True)

def reference(gradient, carried_error, q_start):
    merged_list = [(gradient[g].astype(jnp.float32) + carried_error[g].astype(jnp.float32)).astype(jnp.bfloat16) for g in range(GROUPS)]
    q_factor = q_start
    p_basis = None
    for iteration in range(ITERS):
        q_narrow = q_factor.astype(jnp.bfloat16)
        p_total = jnp.zeros((ROWS, RANK), jnp.float32)
        for g in range(GROUPS):
            p_total = p_total + jnp.dot(merged_list[g].astype(jnp.float32), q_narrow.astype(jnp.float32), preferred_element_type=jnp.float32)
        p_basis = orthonormal(p_total).astype(jnp.bfloat16)
        q_sum = jnp.zeros((COLS, RANK), jnp.float32)
        for g in range(GROUPS):
            q_sum = q_sum + jnp.dot(merged_list[g].T.astype(jnp.float32), p_basis.astype(jnp.float32), preferred_element_type=jnp.float32)
        q_factor = q_sum / GROUPS
    update = jnp.dot(p_basis.astype(jnp.float32), q_factor.T, precision=lax.Precision.HIGHEST)
    errors = []
    for g in range(GROUPS):
        merged_wide = gradient[g].astype(jnp.float32) + carried_error[g].astype(jnp.float32)
        errors.append((merged_wide - update).astype(jnp.bfloat16))
    return (jnp.stack(errors, axis=0), q_factor)
```

```python
import jax
import jax.numpy as jnp
from jax import lax
from jax.experimental import pallas as pl
from jax.experimental.pallas import tpu as pltpu
from jax.sharding import PartitionSpec as P

ITERS = 3
PANEL = 16
HIGHEST = lax.Precision.HIGHEST


def factor_kernel(both_ref, inverse_ref, work):
    rank = inverse_ref.shape[0]
    first_gram = both_ref.shape[0] - rank
    row_id = lax.broadcasted_iota(jnp.int32, (rank, rank), 0)
    col_id = lax.broadcasted_iota(jnp.int32, (rank, rank), 1)
    work[:, :rank] = both_ref[first_gram:, :]
    work[:, rank:] = jnp.where(row_id == col_id, 1.0, 0.0).astype(jnp.float32)
    local = lax.broadcasted_iota(jnp.int32, (PANEL, rank), 0)
    for first in range(0, rank, PANEL):
        left, right = work[first:first + PANEL, :rank], work[first:first + PANEL, rank:]
        columns = [
            jnp.broadcast_to(left[:, first + j:first + j + 1], (PANEL, rank)) for j in range(PANEL)
        ]
        for j in range(PANEL):
            scale = lax.rsqrt(columns[j][j:j + 1, :])
            below = jnp.where(local > j, columns[j] * scale, 0.0)
            row_left, row_right = left[j:j + 1, :] * scale, right[j:j + 1, :] * scale
            left = jnp.where(local == j, row_left, left - below * row_left)
            right = jnp.where(local == j, row_right, right - below * row_right)
            for m in range(j + 1, PANEL):
                columns[m] = columns[m] - below * (columns[m][j:j + 1, :] * scale)
        inverse_ref[first:first + PANEL, :] = right
        rest = first + PANEL
        if rest < rank:
            change = lax.dot_general(
                left, jnp.concatenate([left, right], axis=1), (((0,), (0,)), ((), ())),
                precision=HIGHEST, preferred_element_type=jnp.float32,
            )
            work[rest:, :] = work[rest:, :] - change[rest:, :]


def inverse_factor(both):
    rank = both.shape[1]
    return pl.pallas_call(
        factor_kernel,
        out_shape=jax.ShapeDtypeStruct((rank, rank), jnp.float32),
        in_specs=[pl.BlockSpec(memory_space=pltpu.VMEM)],
        out_specs=pl.BlockSpec(memory_space=pltpu.VMEM),
        scratch_shapes=[pltpu.VMEM((rank, 2 * rank), jnp.float32)],
        name="inverse_factor",
    )(both)


def exchange_sum(rows, axis):
    size = lax.axis_size(axis)
    count, width = rows.shape
    parts = lax.all_to_all(rows.reshape(size, count // size, width), axis, 0, 0)
    total = jnp.sum(parts, axis=0)
    whole = lax.all_to_all(jnp.broadcast_to(total[None], (size,) + total.shape), axis, 0, 0)
    return whole.reshape(count, width)


def group_sum(gradient, carried_error):
    size, here = lax.axis_size("dp"), lax.axis_index("dp")
    count = gradient.shape[0] // size
    half, reach = count // 2, size // 2
    ways = (1, -1)
    rings = {way: [(i, (i + way) % size) for i in range(size)] for way in ways}

    def own(step, part):
        start = lax.rem(here + step + size, size) * count + part * half
        cut = lambda array: lax.dynamic_slice_in_dim(array, start, half).astype(jnp.float32)
        return (cut(gradient) + cut(carried_error)).astype(jnp.bfloat16).astype(jnp.float32)

    def send(values):
        values = lax.optimization_barrier({way: value.astype(jnp.bfloat16) for way, value in values.items()})
        return values, {way: lax.ppermute(value, "dp", rings[way]) for way, value in values.items()}

    flying = [None, None]
    for part, way in enumerate(ways):
        _, flying[part] = send({way: own(way * reach, part)})
    for step in range(reach - 1, -1, -1):
        for part in range(2):
            got = {way: value.astype(jnp.float32) for way, value in flying[part].items()}
            if step:
                values = {way: got[way] + own(way * step, part) if way in got else own(way * step, part) for way in ways}
                values, flying[part] = send(values)
                flying[1 - part], _ = lax.optimization_barrier((flying[1 - part], values))
            else:
                flying[part] = own(0, part) + got[1] + got[-1]
    return jnp.concatenate(flying)


def body(gradient, carried_error, q_start):
    gradient, carried_error = gradient[0], carried_error[0]
    group_count = lax.axis_size("dp")
    summed = group_sum(gradient, carried_error)
    q_factor = q_start
    for iteration in range(ITERS):
        q_narrow = lax.reduce_precision(q_factor, 8, 7)
        partial_value = jnp.dot(summed, q_narrow, precision=HIGHEST)
        p_rows = exchange_sum(partial_value, "col")
        q_part = lax.dot_general(summed, p_rows, (((0,), (0,)), ((), ())), precision=HIGHEST)
        gram_part = lax.dot_general(p_rows, p_rows, (((0,), (0,)), ((), ())), precision=HIGHEST)
        if iteration == ITERS - 1:
            p_total = lax.all_gather(p_rows, "dp", axis=0, tiled=True)
        both = exchange_sum(jnp.concatenate([q_part, gram_part]), "dp")
        upper = inverse_factor(both).T
        q_factor = jnp.dot(both[:q_part.shape[0]], upper, precision=HIGHEST) / group_count
    p_basis = jnp.dot(p_total, upper, precision=HIGHEST).astype(jnp.bfloat16)
    update = jnp.dot(p_basis.astype(jnp.float32), q_factor.T, precision=HIGHEST)
    merged_wide = gradient.astype(jnp.float32) + carried_error.astype(jnp.float32)
    new_error = (merged_wide - update).astype(jnp.bfloat16)[None]
    return (new_error, q_factor)


def solution(mesh):
    placed = (P("dp", None, "col"), P("dp", None, "col"), P("col", None))
    return jax.shard_map(
        body,
        mesh=mesh,
        in_specs=placed,
        out_specs=(P("dp", None, "col"), P("col", None)),
        check_vma=False,
    )
```

```python
import jax
import jax.numpy as jnp
from jax import lax
from jax.experimental import pallas as pl
from jax.experimental.pallas import tpu as pltpu
from jax.sharding import PartitionSpec as P

ITERS = 3
PANEL = 16
HIGHEST = lax.Precision.HIGHEST
QUAD = 4
HALF = 256
SHARE = 112
FACTOR_FLOPS = 4 << 30


def factor_kernel(place_ref, both_ref, inverse_ref, work):
    rank = inverse_ref.shape[0]
    first_gram = both_ref.shape[0] - rank
    row_id = lax.broadcasted_iota(jnp.int32, (rank, rank), 0)
    col_id = lax.broadcasted_iota(jnp.int32, (rank, rank), 1)
    work[:, :rank] = both_ref[first_gram:, :]
    work[:, rank:] = jnp.where(row_id == col_id, 1.0, 0.0).astype(jnp.float32)
    local = lax.broadcasted_iota(jnp.int32, (PANEL, rank), 0)
    for first in range(0, rank, PANEL):
        left, right = work[first:first + PANEL, :rank], work[first:first + PANEL, rank:]
        columns = [
            jnp.broadcast_to(left[:, first + j:first + j + 1], (PANEL, rank)) for j in range(PANEL)
        ]
        for j in range(PANEL):
            scale = lax.rsqrt(columns[j][j:j + 1, :])
            below = jnp.where(local > j, columns[j] * scale, 0.0)
            row_left, row_right = left[j:j + 1, :] * scale, right[j:j + 1, :] * scale
            left = jnp.where(local == j, row_left, left - below * row_left)
            right = jnp.where(local == j, row_right, right - below * row_right)
            for m in range(j + 1, PANEL):
                columns[m] = columns[m] - below * (columns[m][j:j + 1, :] * scale)
        inverse_ref[first:first + PANEL, :] = right
        rest = first + PANEL
        if rest < rank:
            change = lax.dot_general(
                left, jnp.concatenate([left, right], axis=1), (((0,), (0,)), ((), ())),
                precision=HIGHEST, preferred_element_type=jnp.float32,
            )
            work[rest:, :] = work[rest:, :] - change[rest:, :]


def places():
    quad, core = lax.rem(lax.axis_index("dp"), QUAD), lax.rem(lax.axis_index("col"), 2)
    return jnp.stack([quad, core]).astype(jnp.int32)


def local_call(kernel, shapes, operands, scratch=(), flops=0):
    return pl.pallas_call(
        kernel,
        out_shape=[jax.ShapeDtypeStruct(shape, jnp.float32) for shape in shapes],
        in_specs=[pl.BlockSpec(memory_space=pltpu.SMEM)] + [pl.BlockSpec(memory_space=pltpu.VMEM)] * len(operands),
        out_specs=[pl.BlockSpec(memory_space=pltpu.VMEM)] * len(shapes),
        scratch_shapes=[pltpu.VMEM(shape, jnp.float32) for shape in scratch],
        cost_estimate=pl.CostEstimate(flops=flops, bytes_accessed=1 << 20, transcendentals=0),
        compiler_params=pltpu.CompilerParams(vmem_limit_bytes=12 << 20),
        name=kernel.__name__,
    )(places(), *operands)


def dot(a, b, sides):
    return lax.dot_general(
        a, b, ((sides[0:1], sides[1:2]), ((), ())), precision=HIGHEST, preferred_element_type=jnp.float32
    )


def half_of(side):
    return pl.ds(pl.multiple_of(side * HALF, HALF), HALF)


def place_of(place_ref, step):
    return pl.ds(pl.multiple_of(lax.bitwise_xor(place_ref[0], step) * SHARE, 8), SHARE)


def spread(place_ref, summed_ref, q_narrow, send_ref, keep_ref):
    core = place_ref[1]
    keep_ref[...] = dot(summed_ref[half_of(core), :], q_narrow, (1, 0))
    send_ref[...] = dot(summed_ref[half_of(1 - core), :], q_narrow, (1, 0))


def narrow(values):
    return values.astype(jnp.bfloat16).astype(jnp.float32)


def first_kernel(place_ref, q_ref, summed_ref, send_ref, keep_ref):
    spread(place_ref, summed_ref, narrow(q_ref[...]), send_ref, keep_ref)


def normalise(place_ref, inverse_ref, share_refs, q_ref):
    scale = 1.0 / lax.axis_size("dp")
    for step, share_ref in enumerate(share_refs):
        q_ref[place_of(place_ref, step), :] = dot(share_ref[...], inverse_ref[...], (1, 1)) * scale


def middle_kernel(place_ref, inverse_ref, s0, s1, s2, s3, summed_ref, send_ref, keep_ref, q_ref):
    normalise(place_ref, inverse_ref, (s0, s1, s2, s3), q_ref)
    spread(place_ref, summed_ref, narrow(q_ref[...]), send_ref, keep_ref)


def last_kernel(place_ref, inverse_ref, s0, s1, s2, s3, q_ref):
    normalise(place_ref, inverse_ref, (s0, s1, s2, s3), q_ref)


def column_kernel(place_ref, mine_ref, other_ref, turned_ref, o0, o1, o2, o3, rows, columns):
    core = place_ref[1]
    rows[half_of(core), :] = mine_ref[...]
    rows[half_of(1 - core), :] = other_ref[...]
    gram = dot(rows[...], rows[...], (0, 0))
    columns[...] = dot(turned_ref[...], rows[...], (1, 0))
    for step, out_ref in enumerate((o0, o1, o2, o3)):
        out_ref[:SHARE, :] = columns[place_of(place_ref, step), :]
        out_ref[SHARE:, :] = gram


def update_kernel(place_ref, inverse_ref, q_ref, mine_ref, other_ref, gradient_ref, error_ref, out_ref):
    core = place_ref[1]
    parts, rest = [], q_ref[...]
    for _ in range(3):
        parts.append(rest.astype(jnp.bfloat16))
        rest = rest - parts[-1].astype(jnp.float32)
    for side, half_ref in ((core, mine_ref), (1 - core, other_ref)):
        basis = dot(half_ref[...], inverse_ref[...], (1, 1)).astype(jnp.bfloat16)
        update = sum(
            lax.dot_general(part, basis, (((1,), (1,)), ((), ())), preferred_element_type=jnp.float32)
            for part in parts[::-1]
        )
        where = (slice(None), half_of(side))
        wide = gradient_ref[where].astype(jnp.float32) + error_ref[where].astype(jnp.float32)
        out_ref[where] = (wide - update).astype(jnp.bfloat16)


def apply_update(inverse, q_factor, mine, other, gradient, carried_error):
    columns, rows = gradient.shape
    rank = q_factor.shape[1]
    fixed = lambda shape: pl.BlockSpec(shape, lambda i: (0, 0))
    half = pl.BlockSpec((HALF, rank), lambda i: (i, 0))
    block = pl.BlockSpec((columns, 2 * HALF), lambda i: (0, i))
    return pl.pallas_call(
        update_kernel,
        grid=(rows // (2 * HALF),),
        out_shape=jax.ShapeDtypeStruct((columns, rows), jnp.bfloat16),
        in_specs=[pl.BlockSpec(memory_space=pltpu.SMEM), fixed((rank, rank)), fixed((columns, rank)), half, half, block, block],
        out_specs=block,
        compiler_params=pltpu.CompilerParams(vmem_limit_bytes=32 << 20),
        name="apply_update",
    )(places(), inverse, q_factor, mine, other, gradient, carried_error)


def quad_steps(values, axis, unit):
    size = lax.axis_size(axis)
    return [
        lax.ppermute(value, axis, [(i, i ^ (step * unit)) for i in range(size)])
        for step, value in enumerate(values, 1)
    ]


def quad_sum(own, values, axis, unit):
    one, two, three = quad_steps(values, axis, unit)
    return (own + one) + (two + three)


def swap(value, axis, unit):
    return lax.ppermute(value, axis, [(i, i ^ unit) for i in range(lax.axis_size(axis))])


def group_sum(gradient, carried_error):
    size, here = lax.axis_size("dp"), lax.axis_index("dp")
    reach = size // 2
    ways = (1, -1)
    rings = {way: [(i, (i + way) % size) for i in range(size)] for way in ways}

    def own(step, part):
        start = lax.rem(here + step + size, size) * 2 * HALF + part * HALF
        cut = lambda array: lax.dynamic_slice_in_dim(array, start, HALF, axis=1).astype(jnp.float32)
        return (cut(gradient) + cut(carried_error)).astype(jnp.bfloat16).astype(jnp.float32)

    def send(values):
        values = lax.optimization_barrier({way: value.astype(jnp.bfloat16) for way, value in values.items()})
        return values, {way: lax.ppermute(value, "dp", rings[way]) for way, value in values.items()}

    flying = [None, None]
    for part, way in enumerate(ways):
        _, flying[part] = send({way: own(way * reach, part)})
    for step in range(reach - 1, -1, -1):
        for part in range(2):
            got = {way: value.astype(jnp.float32) for way, value in flying[part].items()}
            if step:
                values = {way: got[way] + own(way * step, part) if way in got else own(way * step, part) for way in ways}
                values, flying[part] = send(values)
                flying[1 - part], _ = lax.optimization_barrier((flying[1 - part], values))
            else:
                flying[part] = own(0, part) + got[1] + got[-1]
    return jnp.concatenate(flying, axis=1)


def body(gradient, carried_error, q_start):
    gradient, carried_error = gradient[0].T, carried_error[0].T
    turned = group_sum(gradient, carried_error)
    summed = turned.T
    rank = q_start.shape[1]
    half_shape, share_shape = (HALF, rank), (SHARE + rank, rank)
    send, keep = local_call(first_kernel, [half_shape] * 2, (q_start, summed))
    for iteration in range(ITERS):
        mine = keep + swap(send, "col", 1)
        mine = quad_sum(mine, [mine] * 3, "col", 8)
        mine = quad_sum(mine, [mine] * 3, "col", 2)
        other = swap(mine, "col", 1)
        if iteration == ITERS - 1:
            all_mine = lax.all_gather(mine, "dp", axis=0, tiled=True)
        own, *others = local_call(
            column_kernel, [share_shape] * 4, (mine, other, turned),
            scratch=[(2 * HALF, rank), (QUAD * SHARE, rank)],
        )
        both = quad_sum(own, others, "dp", 1)
        both = both + swap(both, "dp", QUAD)
        share = both[:SHARE]
        shares = [share] + quad_steps([share] * 3, "dp", 1)
        if iteration == ITERS - 1:
            all_mine, shares = lax.optimization_barrier((all_mine, shares))
            all_other = swap(all_mine, "col", 1)
        inverse, = local_call(factor_kernel, [(rank, rank)], (both,), scratch=[(rank, 2 * rank)], flops=FACTOR_FLOPS)
        if iteration < ITERS - 1:
            send, keep, _ = local_call(
                middle_kernel, [half_shape] * 2 + [q_start.shape], (inverse, *shares, summed)
            )
    q_factor, = local_call(last_kernel, [q_start.shape], (inverse, *shares))
    new_error = apply_update(inverse, q_factor, all_mine, all_other, gradient, carried_error)
    return (new_error.T[None], q_factor)


def solution(mesh):
    placed = (P("dp", None, "col"), P("dp", None, "col"), P("col", None))
    return jax.shard_map(
        body,
        mesh=mesh,
        in_specs=placed,
        out_specs=(P("dp", None, "col"), P("col", None)),
        check_vma=False,
    )
```

```python
import jax
import jax.numpy as jnp
from jax import lax
from jax.experimental import pallas as pl
from jax.experimental.pallas import tpu as pltpu
from jax.sharding import PartitionSpec as P

ITERS = 3
PANEL = 16
HIGHEST = lax.Precision.HIGHEST
QUAD = 4
HALF = 256
SHARE = 112
SLICE = 32
FACTOR_FLOPS = 4 << 30


def factor(place_ref, share_refs, inverse_ref, work):
    rank = inverse_ref.shape[0]
    row_id = lax.broadcasted_iota(jnp.int32, (rank, rank), 0)
    col_id = lax.broadcasted_iota(jnp.int32, (rank, rank), 1)
    for step, share_ref in enumerate(share_refs):
        work[place_of(place_ref, step, SLICE), :rank] = share_ref[SHARE:, :]
    work[:, rank:] = jnp.where(row_id == col_id, 1.0, 0.0).astype(jnp.float32)
    local = lax.broadcasted_iota(jnp.int32, (PANEL, rank), 0)
    for first in range(0, rank, PANEL):
        left, right = work[first:first + PANEL, :rank], work[first:first + PANEL, rank:]
        columns = [
            jnp.broadcast_to(left[:, first + j:first + j + 1], (PANEL, rank)) for j in range(PANEL)
        ]
        for j in range(PANEL):
            scale = lax.rsqrt(columns[j][j:j + 1, :])
            below = jnp.where(local > j, columns[j] * scale, 0.0)
            row_left, row_right = left[j:j + 1, :] * scale, right[j:j + 1, :] * scale
            left = jnp.where(local == j, row_left, left - below * row_left)
            right = jnp.where(local == j, row_right, right - below * row_right)
            for m in range(j + 1, PANEL):
                columns[m] = columns[m] - below * (columns[m][j:j + 1, :] * scale)
        inverse_ref[first:first + PANEL, :] = right
        rest = first + PANEL
        if rest < rank:
            change = lax.dot_general(
                left, jnp.concatenate([left, right], axis=1), (((0,), (0,)), ((), ())),
                precision=HIGHEST, preferred_element_type=jnp.float32,
            )
            work[rest:, :] = work[rest:, :] - change[rest:, :]


def places():
    quad, core = lax.rem(lax.axis_index("dp"), QUAD), lax.rem(lax.axis_index("col"), 2)
    return jnp.stack([quad, core, lax.axis_index("dp")]).astype(jnp.int32)


def local_call(kernel, shapes, operands, scratch=(), flops=0):
    return pl.pallas_call(
        kernel,
        out_shape=[jax.ShapeDtypeStruct(shape, jnp.float32) for shape in shapes],
        in_specs=[pl.BlockSpec(memory_space=pltpu.SMEM)] + [pl.BlockSpec(memory_space=pltpu.VMEM)] * len(operands),
        out_specs=[pl.BlockSpec(memory_space=pltpu.VMEM)] * len(shapes),
        scratch_shapes=[pltpu.VMEM(shape, jnp.float32) for shape in scratch],
        cost_estimate=pl.CostEstimate(flops=flops, bytes_accessed=1 << 20, transcendentals=0),
        compiler_params=pltpu.CompilerParams(vmem_limit_bytes=12 << 20),
        name=kernel.__name__,
    )(places(), *operands)


def dot(a, b, sides):
    return lax.dot_general(
        a, b, ((sides[0:1], sides[1:2]), ((), ())), precision=HIGHEST, preferred_element_type=jnp.float32
    )


def half_of(side):
    return pl.ds(pl.multiple_of(side * HALF, HALF), HALF)


def place_of(place_ref, step, count):
    return pl.ds(pl.multiple_of(lax.bitwise_xor(place_ref[0], step) * count, 8), count)


def spread(place_ref, summed_ref, q_narrow, send_ref, keep_ref):
    core = place_ref[1]
    keep_ref[...] = dot(summed_ref[half_of(core), :], q_narrow, (1, 0))
    send_ref[...] = dot(summed_ref[half_of(1 - core), :], q_narrow, (1, 0))


def narrow(values):
    return values.astype(jnp.bfloat16).astype(jnp.float32)


def first_kernel(place_ref, q_ref, summed_ref, send_ref, keep_ref):
    spread(place_ref, summed_ref, narrow(q_ref[...]), send_ref, keep_ref)


def normalise(place_ref, share_refs, inverse_ref, q_ref, work):
    factor(place_ref, share_refs, inverse_ref, work)
    scale = 1.0 / lax.axis_size("dp")
    for step, share_ref in enumerate(share_refs):
        q_ref[place_of(place_ref, step, SHARE), :] = dot(share_ref[:SHARE, :], inverse_ref[...], (1, 1)) * scale


def middle_kernel(place_ref, s0, s1, s2, s3, summed_ref, send_ref, keep_ref, inverse, q, work):
    normalise(place_ref, (s0, s1, s2, s3), inverse, q, work)
    spread(place_ref, summed_ref, narrow(q[...]), send_ref, keep_ref)


def last_kernel(place_ref, s0, s1, s2, s3, upper_ref, q_ref, inverse, work):
    normalise(place_ref, (s0, s1, s2, s3), inverse, q_ref, work)
    upper_ref[...] = inverse[...].T


def column_kernel(place_ref, mine_ref, other_ref, turned_ref, o0, o1, o2, o3, rows, columns, gram):
    core = place_ref[1]
    rows[half_of(core), :] = mine_ref[...]
    rows[half_of(1 - core), :] = other_ref[...]
    gram[...] = dot(rows[...], rows[...], (0, 0))
    columns[...] = dot(turned_ref[...], rows[...], (1, 0))
    for step, out_ref in enumerate((o0, o1, o2, o3)):
        out_ref[:SHARE, :] = columns[place_of(place_ref, step, SHARE), :]
        out_ref[SHARE:, :] = gram[place_of(place_ref, step, SLICE), :]


def halves_of(values, count):
    parts = []
    for _ in range(count):
        parts.append(values.astype(jnp.bfloat16))
        values = values - parts[-1].astype(jnp.float32)
    return parts


def update_kernel(place_ref, upper_ref, q_ref, mine_ref, other_ref, gradient_ref, error_ref, out_ref):
    core = place_ref[1]
    q_high, q_low = halves_of(q_ref[...], 2)
    q_wide = jnp.concatenate([q_high, q_low], axis=1)
    u_high, u_middle, u_low = halves_of(upper_ref[...], 3)
    times = lambda a, b, c, d: jnp.dot(
        jnp.concatenate([a, b], axis=1), jnp.concatenate([c, d]), preferred_element_type=jnp.float32
    )
    for side, half_ref in ((core, mine_ref), (1 - core, other_ref)):
        high, middle, low = halves_of(half_ref[...], 3)
        basis = times(high, low, u_low, u_high) + times(high, middle, u_middle, u_middle)
        basis = (basis + times(high, middle, u_high, u_high)).astype(jnp.bfloat16)
        update = lax.dot_general(
            q_wide, jnp.concatenate([basis, basis], axis=1), (((1,), (1,)), ((), ())),
            preferred_element_type=jnp.float32,
        )
        where = (slice(None), half_of(side))
        wide = gradient_ref[where].astype(jnp.float32) + error_ref[where].astype(jnp.float32)
        out_ref[where] = (wide - update).astype(jnp.bfloat16)


def apply_update(upper, q_factor, mine, other, gradient, carried_error):
    columns, rows = gradient.shape
    rank = q_factor.shape[1]
    groups = lax.axis_size("dp")
    fixed = lambda shape: pl.BlockSpec(shape, lambda i, place: (0, 0))
    half = pl.BlockSpec((HALF, rank), lambda i, place: (i, 0))
    block = pl.BlockSpec((columns, 2 * HALF), lambda i, place: (0, lax.rem(place[2] + i, groups)))
    return pl.pallas_call(
        update_kernel,
        grid_spec=pltpu.PrefetchScalarGridSpec(
            num_scalar_prefetch=1,
            grid=(groups,),
            in_specs=[fixed((rank, rank)), fixed((columns, rank)), half, half, block, block],
            out_specs=block,
        ),
        out_shape=jax.ShapeDtypeStruct((columns, rows), jnp.bfloat16),
        compiler_params=pltpu.CompilerParams(vmem_limit_bytes=32 << 20),
        name="apply_update",
    )(places(), upper, q_factor, mine, other, gradient, carried_error)


def quad_steps(values, axis, unit):
    size = lax.axis_size(axis)
    return [
        lax.ppermute(value, axis, [(i, i ^ (step * unit)) for i in range(size)])
        for step, value in enumerate(values, 1)
    ]


def quad_sum(own, values, axis, unit):
    one, two, three = quad_steps(values, axis, unit)
    return (own + one) + (two + three)


def swap(value, axis, unit):
    return lax.ppermute(value, axis, [(i, i ^ unit) for i in range(lax.axis_size(axis))])


def ring_step(values):
    size = lax.axis_size("dp")
    return {way: lax.ppermute(value, "dp", [(i, (i + way) % size) for i in range(size)]) for way, value in values.items()}


def group_sum(gradient, carried_error):
    size, here = lax.axis_size("dp"), lax.axis_index("dp")
    reach = size // 2
    ways = (1, -1)
    rings = {way: [(i, (i + way) % size) for i in range(size)] for way in ways}

    def own(step, part):
        start = lax.rem(here + step + size, size) * 2 * HALF + part * HALF
        cut = lambda array: lax.dynamic_slice_in_dim(array, start, HALF, axis=1).astype(jnp.float32)
        return (cut(gradient) + cut(carried_error)).astype(jnp.bfloat16).astype(jnp.float32)

    def send(values):
        values = lax.optimization_barrier({way: value.astype(jnp.bfloat16) for way, value in values.items()})
        return values, {way: lax.ppermute(value, "dp", rings[way]) for way, value in values.items()}

    flying = [None, None]
    for part, way in enumerate(ways):
        _, flying[part] = send({way: own(way * reach, part)})
    for step in range(reach - 1, -1, -1):
        for part in range(2):
            got = {way: value.astype(jnp.float32) for way, value in flying[part].items()}
            if step:
                values = {way: got[way] + own(way * step, part) if way in got else own(way * step, part) for way in ways}
                values, flying[part] = send(values)
                flying[1 - part], _ = lax.optimization_barrier((flying[1 - part], values))
            else:
                flying[part] = own(0, part) + got[1] + got[-1]
    return jnp.concatenate(flying, axis=1)


def body(gradient, carried_error, q_start):
    gradient, carried_error = gradient[0].T, carried_error[0].T
    turned = group_sum(gradient, carried_error)
    summed = turned.T
    rank = q_start.shape[1]
    half_shape, share_shape, square = (HALF, rank), (SHARE + SLICE, rank), (rank, rank)
    send, keep = local_call(first_kernel, [half_shape] * 2, (q_start, summed))
    for iteration in range(ITERS):
        mine = keep + swap(send, "col", 1)
        mine = quad_sum(mine, [mine] * 3, "col", 8)
        mine = quad_sum(mine, [mine] * 3, "col", 2)
        other = swap(mine, "col", 1)
        last = iteration == ITERS - 1
        if last:
            flying = ring_step({1: mine, -1: mine})
        own, *others = local_call(
            column_kernel, [share_shape] * 4, (mine, other, turned),
            scratch=[(2 * HALF, rank), (QUAD * SHARE, rank), square],
        )
        share = quad_sum(own, others, "dp", 1)
        if last:
            (near, mine, share) = lax.optimization_barrier((flying, mine, share))
            flying = ring_step(near)
            across = swap(mine, "dp", QUAD)
        share = share + swap(share, "dp", QUAD)
        if last:
            (middle, across, share) = lax.optimization_barrier((flying, across, share))
            flying = ring_step(middle)
        shares = [share] + quad_steps([share] * 3, "dp", 1)
        if iteration < ITERS - 1:
            send, keep = local_call(
                middle_kernel, [half_shape] * 2, (*shares, summed),
                scratch=[square, q_start.shape, (rank, 2 * rank)],
            )
    far, shares = lax.optimization_barrier((flying, shares))
    blocks = [mine, near[-1], middle[-1], far[-1], across, far[1], middle[1], near[1]]
    all_mine = jnp.concatenate(blocks)
    all_other = jnp.concatenate([other] + [swap(block, "col", 1) for block in blocks[1:]])
    upper, q_factor = local_call(
        last_kernel, [square, q_start.shape], shares, scratch=[square, (rank, 2 * rank)], flops=FACTOR_FLOPS
    )
    new_error = apply_update(upper, q_factor, all_mine, all_other, gradient, carried_error)
    return (new_error.T[None], q_factor)


def solution(mesh):
    placed = (P("dp", None, "col"), P("dp", None, "col"), P("col", None))
    return jax.shard_map(
        body,
        mesh=mesh,
        in_specs=placed,
        out_specs=(P("dp", None, "col"), P("col", None)),
        check_vma=False,
    )
```

```python
import jax
import jax.numpy as jnp
from jax import lax
from jax.experimental import pallas as pl
from jax.experimental.pallas import tpu as pltpu
from jax.sharding import PartitionSpec as P

ITERS = 3
PANEL = 16
HIGHEST = lax.Precision.HIGHEST
QUAD = 4
HALF = 256
SHARE = 112
SLICE = 32
FACTOR_FLOPS = 4 << 30


def factor(place_ref, share_refs, inverse_ref, work):
    rank = inverse_ref.shape[0]
    row_id = lax.broadcasted_iota(jnp.int32, (rank, rank), 0)
    col_id = lax.broadcasted_iota(jnp.int32, (rank, rank), 1)
    for step, share_ref in enumerate(share_refs):
        work[place_of(place_ref, step, SLICE), :rank] = share_ref[SHARE:, :]
    work[:, rank:] = jnp.where(row_id == col_id, 1.0, 0.0).astype(jnp.float32)
    local = lax.broadcasted_iota(jnp.int32, (PANEL, rank), 0)
    for first in range(0, rank, PANEL):
        left, right = work[first:first + PANEL, :rank], work[first:first + PANEL, rank:]
        columns = [
            jnp.broadcast_to(left[:, first + j:first + j + 1], (PANEL, rank)) for j in range(PANEL)
        ]
        for j in range(PANEL):
            scale = lax.rsqrt(columns[j][j:j + 1, :])
            below = jnp.where(local > j, columns[j] * scale, 0.0)
            row_left, row_right = left[j:j + 1, :] * scale, right[j:j + 1, :] * scale
            left = jnp.where(local == j, row_left, left - below * row_left)
            right = jnp.where(local == j, row_right, right - below * row_right)
            for m in range(j + 1, PANEL):
                columns[m] = columns[m] - below * (columns[m][j:j + 1, :] * scale)
        inverse_ref[first:first + PANEL, :] = right
        rest = first + PANEL
        if rest < rank:
            change = lax.dot_general(
                left, jnp.concatenate([left, right], axis=1), (((0,), (0,)), ((), ())),
                precision=HIGHEST, preferred_element_type=jnp.float32,
            )
            work[rest:, :] = work[rest:, :] - change[rest:, :]


def places():
    quad, core = lax.rem(lax.axis_index("dp"), QUAD), lax.rem(lax.axis_index("col"), 2)
    return jnp.stack([quad, core, lax.axis_index("dp")]).astype(jnp.int32)


def local_call(kernel, shapes, operands, scratch=(), flops=0):
    return pl.pallas_call(
        kernel,
        out_shape=[jax.ShapeDtypeStruct(shape, jnp.float32) for shape in shapes],
        in_specs=[pl.BlockSpec(memory_space=pltpu.SMEM)] + [pl.BlockSpec(memory_space=pltpu.VMEM)] * len(operands),
        out_specs=[pl.BlockSpec(memory_space=pltpu.VMEM)] * len(shapes),
        scratch_shapes=[pltpu.VMEM(shape, jnp.float32) for shape in scratch],
        cost_estimate=pl.CostEstimate(flops=flops, bytes_accessed=1 << 20, transcendentals=0),
        compiler_params=pltpu.CompilerParams(vmem_limit_bytes=12 << 20),
        name=kernel.__name__,
    )(places(), *operands)


def dot(a, b, sides):
    return lax.dot_general(
        a, b, ((sides[0:1], sides[1:2]), ((), ())), precision=HIGHEST, preferred_element_type=jnp.float32
    )


def half_of(side):
    return pl.ds(pl.multiple_of(side * HALF, HALF), HALF)


def place_of(place_ref, step, count):
    return pl.ds(pl.multiple_of(lax.bitwise_xor(place_ref[0], step) * count, 8), count)


def spread(place_ref, summed_ref, q_narrow, send_ref, keep_ref):
    core = place_ref[1]
    keep_ref[...] = dot(summed_ref[half_of(core), :], q_narrow, (1, 0))
    send_ref[...] = dot(summed_ref[half_of(1 - core), :], q_narrow, (1, 0))


def narrow(values):
    return values.astype(jnp.bfloat16).astype(jnp.float32)


def first_kernel(place_ref, q_ref, summed_ref, send_ref, keep_ref):
    spread(place_ref, summed_ref, narrow(q_ref[...]), send_ref, keep_ref)


def normalise(place_ref, share_refs, inverse_ref, q_ref, work):
    factor(place_ref, share_refs, inverse_ref, work)
    scale = 1.0 / lax.axis_size("dp")
    for step, share_ref in enumerate(share_refs):
        q_ref[place_of(place_ref, step, SHARE), :] = dot(share_ref[:SHARE, :], inverse_ref[...], (1, 1)) * scale


def middle_kernel(place_ref, s0, s1, s2, s3, summed_ref, send_ref, keep_ref, inverse, q, work):
    normalise(place_ref, (s0, s1, s2, s3), inverse, q, work)
    spread(place_ref, summed_ref, narrow(q[...]), send_ref, keep_ref)


def last_kernel(place_ref, s0, s1, s2, s3, upper_ref, q_ref, inverse, work):
    normalise(place_ref, (s0, s1, s2, s3), inverse, q_ref, work)
    upper_ref[...] = inverse[...].T


def column_kernel(place_ref, mine_ref, other_ref, turned_ref, o0, o1, o2, o3, rows, columns, gram):
    core = place_ref[1]
    rows[half_of(core), :] = mine_ref[...]
    rows[half_of(1 - core), :] = other_ref[...]
    gram[...] = dot(rows[...], rows[...], (0, 0))
    columns[...] = dot(turned_ref[...], rows[...], (1, 0))
    for step, out_ref in enumerate((o0, o1, o2, o3)):
        out_ref[:SHARE, :] = columns[place_of(place_ref, step, SHARE), :]
        out_ref[SHARE:, :] = gram[place_of(place_ref, step, SLICE), :]


def halves_of(values, count):
    parts = []
    for _ in range(count):
        parts.append(values.astype(jnp.bfloat16))
        values = values - parts[-1].astype(jnp.float32)
    return parts


def update_kernel(place_ref, upper_ref, q_ref, mine_ref, other_ref, gradient_ref, error_ref, out_ref):
    core = place_ref[1]
    q_high, q_low = halves_of(q_ref[...], 2)
    q_wide = jnp.concatenate([q_high, q_low], axis=1)
    u_high, u_middle, u_low = halves_of(upper_ref[...], 3)
    times = lambda a, b, c, d: jnp.dot(
        jnp.concatenate([a, b], axis=1), jnp.concatenate([c, d]), preferred_element_type=jnp.float32
    )
    for side, half_ref in ((core, mine_ref), (1 - core, other_ref)):
        high, middle, low = halves_of(half_ref[...], 3)
        basis = times(high, low, u_low, u_high) + times(high, middle, u_middle, u_middle)
        basis = (basis + times(high, middle, u_high, u_high)).astype(jnp.bfloat16)
        update = lax.dot_general(
            q_wide, jnp.concatenate([basis, basis], axis=1), (((1,), (1,)), ((), ())),
            preferred_element_type=jnp.float32,
        )
        where = (slice(None), half_of(side))
        wide = gradient_ref[where].astype(jnp.float32) + error_ref[where].astype(jnp.float32)
        out_ref[where] = (wide - update).astype(jnp.bfloat16)


def apply_update(upper, q_factor, mine, other, gradient, carried_error):
    columns, rows = gradient.shape
    rank = q_factor.shape[1]
    groups = lax.axis_size("dp")
    fixed = lambda shape: pl.BlockSpec(shape, lambda i, place: (0, 0))
    half = pl.BlockSpec((HALF, rank), lambda i, place: (i, 0))
    block = pl.BlockSpec((columns, 2 * HALF), lambda i, place: (0, lax.rem(place[2] + i, groups)))
    return pl.pallas_call(
        update_kernel,
        grid_spec=pltpu.PrefetchScalarGridSpec(
            num_scalar_prefetch=1,
            grid=(groups,),
            in_specs=[fixed((rank, rank)), fixed((columns, rank)), half, half, block, block],
            out_specs=block,
        ),
        out_shape=jax.ShapeDtypeStruct((columns, rows), jnp.bfloat16),
        compiler_params=pltpu.CompilerParams(vmem_limit_bytes=32 << 20),
        name="apply_update",
    )(places(), upper, q_factor, mine, other, gradient, carried_error)


def quad_steps(values, axis, unit):
    size = lax.axis_size(axis)
    return [
        lax.ppermute(value, axis, [(i, i ^ (step * unit)) for i in range(size)])
        for step, value in enumerate(values, 1)
    ]


def quad_sum(own, values, axis, unit):
    one, two, three = quad_steps(values, axis, unit)
    return (own + one) + (two + three)


def swap(value, axis, unit):
    return lax.ppermute(value, axis, [(i, i ^ unit) for i in range(lax.axis_size(axis))])


def ring_step(values):
    size = lax.axis_size("dp")
    return {way: lax.ppermute(value, "dp", [(i, (i + way) % size) for i in range(size)]) for way, value in values.items()}


def group_sum(gradient, carried_error):
    size, here = lax.axis_size("dp"), lax.axis_index("dp")
    reach = size // 2
    ways = (1, -1)
    rings = {way: [(i, (i + way) % size) for i in range(size)] for way in ways}

    def own(step, part):
        start = lax.rem(here + step + size, size) * 2 * HALF + part * HALF
        cut = lambda array: lax.dynamic_slice_in_dim(array, start, HALF, axis=1).astype(jnp.float32)
        return (cut(gradient) + cut(carried_error)).astype(jnp.bfloat16).astype(jnp.float32)

    def send(values):
        values = lax.optimization_barrier({way: value.astype(jnp.bfloat16) for way, value in values.items()})
        return values, {way: lax.ppermute(value, "dp", rings[way]) for way, value in values.items()}

    flying = [None, None]
    for part, way in enumerate(ways):
        _, flying[part] = send({way: own(way * reach, part)})
    for step in range(reach - 1, -1, -1):
        for part in range(2):
            got = {way: value.astype(jnp.float32) for way, value in flying[part].items()}
            if step:
                values = {way: got[way] + own(way * step, part) if way in got else own(way * step, part) for way in ways}
                values, flying[part] = send(values)
                flying[1 - part], _ = lax.optimization_barrier((flying[1 - part], values))
            else:
                flying[part] = own(0, part) + got[1] + got[-1]
    return jnp.concatenate(flying, axis=1)


def body(gradient, carried_error, q_start):
    gradient, carried_error = gradient[0].T, carried_error[0].T
    turned = group_sum(gradient, carried_error)
    summed = turned.T
    rank = q_start.shape[1]
    half_shape, share_shape, square = (HALF, rank), (SHARE + SLICE, rank), (rank, rank)
    send, keep = local_call(first_kernel, [half_shape] * 2, (q_start, summed))
    for iteration in range(ITERS):
        mine = keep + swap(send, "col", 1)
        mine = quad_sum(mine, [mine] * 3, "col", 8)
        mine = quad_sum(mine, [mine] * 3, "col", 2)
        other = swap(mine, "col", 1)
        last = iteration == ITERS - 1
        if last:
            flying = ring_step({1: mine, -1: mine})
        own, *others = local_call(
            column_kernel, [share_shape] * 4, (mine, other, turned),
            scratch=[(2 * HALF, rank), (QUAD * SHARE, rank), square],
        )
        share = quad_sum(own, others, "dp", 1)
        if last:
            (near, share) = lax.optimization_barrier((flying, share))
            flying = ring_step(near)
        share = share + swap(share, "dp", QUAD)
        if last:
            (middle, mine, share) = lax.optimization_barrier((flying, mine, share))
            flying = ring_step(middle)
            across = swap(mine, "dp", QUAD)
        shares = [share] + quad_steps([share] * 3, "dp", 1)
        if iteration < ITERS - 1:
            send, keep = local_call(
                middle_kernel, [half_shape] * 2, (*shares, summed),
                scratch=[square, q_start.shape, (rank, 2 * rank)],
            )
    far, across, shares = lax.optimization_barrier((flying, across, shares))
    blocks = [mine, near[-1], middle[-1], far[-1], across, far[1], middle[1], near[1]]
    all_mine = jnp.concatenate(blocks)
    all_other = jnp.concatenate([other] + [swap(block, "col", 1) for block in blocks[1:]])
    upper, q_factor = local_call(
        last_kernel, [square, q_start.shape], shares, scratch=[square, (rank, 2 * rank)], flops=FACTOR_FLOPS
    )
    new_error = apply_update(upper, q_factor, all_mine, all_other, gradient, carried_error)
    return (new_error.T[None], q_factor)


def solution(mesh):
    placed = (P("dp", None, "col"), P("dp", None, "col"), P("col", None))
    return jax.shard_map(
        body,
        mesh=mesh,
        in_specs=placed,
        out_specs=(P("dp", None, "col"), P("col", None)),
        check_vma=False,
    )
```

```python
import jax
import jax.numpy as jnp
from jax import lax
from jax.experimental import pallas as pl
from jax.experimental.pallas import tpu as pltpu
from jax.sharding import PartitionSpec as P

ITERS = 3
PANEL = 16
HIGHEST = lax.Precision.HIGHEST
QUAD = 4
HALF = 256
SHARE = 112
SLICE = 32
FACTOR_FLOPS = 4 << 30


def factor(place_ref, share_refs, inverse_ref, work):
    rank = inverse_ref.shape[0]
    row_id = lax.broadcasted_iota(jnp.int32, (rank, rank), 0)
    col_id = lax.broadcasted_iota(jnp.int32, (rank, rank), 1)
    for step, share_ref in enumerate(share_refs):
        work[place_of(place_ref, step, SLICE), :rank] = share_ref[SHARE:, :]
    work[:, rank:] = jnp.where(row_id == col_id, 1.0, 0.0).astype(jnp.float32)
    local = lax.broadcasted_iota(jnp.int32, (PANEL, rank), 0)
    for first in range(0, rank, PANEL):
        left, right = work[first:first + PANEL, :rank], work[first:first + PANEL, rank:]
        columns = [
            jnp.broadcast_to(left[:, first + j:first + j + 1], (PANEL, rank)) for j in range(PANEL)
        ]
        for j in range(PANEL):
            scale = lax.rsqrt(columns[j][j:j + 1, :])
            below = jnp.where(local > j, columns[j] * scale, 0.0)
            row_left, row_right = left[j:j + 1, :] * scale, right[j:j + 1, :] * scale
            left = jnp.where(local == j, row_left, left - below * row_left)
            right = jnp.where(local == j, row_right, right - below * row_right)
            for m in range(j + 1, PANEL):
                columns[m] = columns[m] - below * (columns[m][j:j + 1, :] * scale)
        inverse_ref[first:first + PANEL, :] = right
        rest = first + PANEL
        if rest < rank:
            change = lax.dot_general(
                left, jnp.concatenate([left, right], axis=1), (((0,), (0,)), ((), ())),
                precision=HIGHEST, preferred_element_type=jnp.float32,
            )
            work[rest:, :] = work[rest:, :] - change[rest:, :]


def places():
    quad, core = lax.rem(lax.axis_index("dp"), QUAD), lax.rem(lax.axis_index("col"), 2)
    return jnp.stack([quad, core, lax.axis_index("dp")]).astype(jnp.int32)


def local_call(kernel, shapes, operands, scratch=(), flops=0):
    return pl.pallas_call(
        kernel,
        out_shape=[jax.ShapeDtypeStruct(shape, jnp.float32) for shape in shapes],
        in_specs=[pl.BlockSpec(memory_space=pltpu.SMEM)] + [pl.BlockSpec(memory_space=pltpu.VMEM)] * len(operands),
        out_specs=[pl.BlockSpec(memory_space=pltpu.VMEM)] * len(shapes),
        scratch_shapes=[pltpu.VMEM(shape, jnp.float32) for shape in scratch],
        cost_estimate=pl.CostEstimate(flops=flops, bytes_accessed=1 << 20, transcendentals=0),
        compiler_params=pltpu.CompilerParams(vmem_limit_bytes=12 << 20),
        name=kernel.__name__,
    )(places(), *operands)


def dot(a, b, sides):
    return lax.dot_general(
        a, b, ((sides[0:1], sides[1:2]), ((), ())), precision=HIGHEST, preferred_element_type=jnp.float32
    )


def half_of(side):
    return pl.ds(pl.multiple_of(side * HALF, HALF), HALF)


def place_of(place_ref, step, count):
    return pl.ds(pl.multiple_of(lax.bitwise_xor(place_ref[0], step) * count, 8), count)


def spread(place_ref, summed_ref, q_narrow, send_ref, keep_ref):
    core = place_ref[1]
    keep_ref[...] = dot(summed_ref[half_of(core), :], q_narrow, (1, 0))
    send_ref[...] = dot(summed_ref[half_of(1 - core), :], q_narrow, (1, 0))


def narrow(values):
    return values.astype(jnp.bfloat16).astype(jnp.float32)


def first_kernel(place_ref, q_ref, summed_ref, send_ref, keep_ref):
    spread(place_ref, summed_ref, narrow(q_ref[...]), send_ref, keep_ref)


def normalise(place_ref, share_refs, inverse_ref, q_ref, work):
    factor(place_ref, share_refs, inverse_ref, work)
    scale = 1.0 / lax.axis_size("dp")
    for step, share_ref in enumerate(share_refs):
        q_ref[place_of(place_ref, step, SHARE), :] = dot(share_ref[:SHARE, :], inverse_ref[...], (1, 1)) * scale


def middle_kernel(place_ref, s0, s1, s2, s3, summed_ref, send_ref, keep_ref, inverse, q, work):
    normalise(place_ref, (s0, s1, s2, s3), inverse, q, work)
    spread(place_ref, summed_ref, narrow(q[...]), send_ref, keep_ref)


def last_kernel(place_ref, s0, s1, s2, s3, upper_ref, q_ref, inverse, work):
    normalise(place_ref, (s0, s1, s2, s3), inverse, q_ref, work)
    upper_ref[...] = inverse[...].T


def column_kernel(place_ref, mine_ref, other_ref, turned_ref, o0, o1, o2, o3, rows, columns, gram):
    core = place_ref[1]
    rows[half_of(core), :] = mine_ref[...]
    rows[half_of(1 - core), :] = other_ref[...]
    gram[...] = dot(rows[...], rows[...], (0, 0))
    columns[...] = dot(turned_ref[...], rows[...], (1, 0))
    for step, out_ref in enumerate((o0, o1, o2, o3)):
        out_ref[:SHARE, :] = columns[place_of(place_ref, step, SHARE), :]
        out_ref[SHARE:, :] = gram[place_of(place_ref, step, SLICE), :]


def halves_of(values, count):
    parts = []
    for _ in range(count):
        parts.append(values.astype(jnp.bfloat16))
        values = values - parts[-1].astype(jnp.float32)
    return parts


def update_kernel(place_ref, upper_ref, q_ref, mine_ref, other_ref, gradient_ref, error_ref, out_ref):
    core = place_ref[1]
    q_high, q_low = halves_of(q_ref[...], 2)
    q_wide = jnp.concatenate([q_high, q_low], axis=1)
    u_high, u_middle, u_low = halves_of(upper_ref[...], 3)
    times = lambda a, b, c, d: jnp.dot(
        jnp.concatenate([a, b], axis=1), jnp.concatenate([c, d]), preferred_element_type=jnp.float32
    )
    for side, half_ref in ((core, mine_ref), (1 - core, other_ref)):
        high, middle, low = halves_of(half_ref[...], 3)
        basis = times(high, low, u_low, u_high) + times(high, middle, u_middle, u_middle)
        basis = (basis + times(high, middle, u_high, u_high)).astype(jnp.bfloat16)
        update = lax.dot_general(
            q_wide, jnp.concatenate([basis, basis], axis=1), (((1,), (1,)), ((), ())),
            preferred_element_type=jnp.float32,
        )
        where = (slice(None), half_of(side))
        wide = gradient_ref[where].astype(jnp.float32) + error_ref[where].astype(jnp.float32)
        out_ref[where] = (wide - update).astype(jnp.bfloat16)


def apply_update(upper, q_factor, mine, other, gradient, carried_error):
    columns, rows = gradient.shape
    rank = q_factor.shape[1]
    groups = lax.axis_size("dp")
    fixed = lambda shape: pl.BlockSpec(shape, lambda i, place: (0, 0))
    half = pl.BlockSpec((HALF, rank), lambda i, place: (i, 0))
    block = pl.BlockSpec((columns, 2 * HALF), lambda i, place: (0, lax.rem(place[2] + i, groups)))
    return pl.pallas_call(
        update_kernel,
        grid_spec=pltpu.PrefetchScalarGridSpec(
            num_scalar_prefetch=1,
            grid=(groups,),
            in_specs=[fixed((rank, rank)), fixed((columns, rank)), half, half, block, block],
            out_specs=block,
        ),
        out_shape=jax.ShapeDtypeStruct((columns, rows), jnp.bfloat16),
        compiler_params=pltpu.CompilerParams(vmem_limit_bytes=32 << 20),
        name="apply_update",
    )(places(), upper, q_factor, mine, other, gradient, carried_error)


def quad_steps(values, axis, unit):
    size = lax.axis_size(axis)
    return [
        lax.ppermute(value, axis, [(i, i ^ (step * unit)) for i in range(size)])
        for step, value in enumerate(values, 1)
    ]


def quad_sum(own, values, axis, unit):
    one, two, three = quad_steps(values, axis, unit)
    return (own + one) + (two + three)


def plane_sum(value):
    count = value.shape[0] // 2
    parts = [value[:count], value[count:]]
    for units in ((8, 2), (2, 8)):
        parts = lax.optimization_barrier(parts)
        parts = [quad_sum(part, [part] * 3, "col", unit) for part, unit in zip(parts, units)]
    return jnp.concatenate(parts)


def swap(value, axis, unit):
    return lax.ppermute(value, axis, [(i, i ^ unit) for i in range(lax.axis_size(axis))])


def ring_step(values):
    size = lax.axis_size("dp")
    return {way: lax.ppermute(value, "dp", [(i, (i + way) % size) for i in range(size)]) for way, value in values.items()}


def group_sum(gradient, carried_error):
    size, here = lax.axis_size("dp"), lax.axis_index("dp")
    reach = size // 2
    ways = (1, -1)
    rings = {way: [(i, (i + way) % size) for i in range(size)] for way in ways}

    def own(step, part):
        start = lax.rem(here + step + size, size) * 2 * HALF + part * HALF
        cut = lambda array: lax.dynamic_slice_in_dim(array, start, HALF, axis=1).astype(jnp.float32)
        return (cut(gradient) + cut(carried_error)).astype(jnp.bfloat16).astype(jnp.float32)

    def send(values):
        values = lax.optimization_barrier({way: value.astype(jnp.bfloat16) for way, value in values.items()})
        return values, {way: lax.ppermute(value, "dp", rings[way]) for way, value in values.items()}

    flying = [None, None]
    for part, way in enumerate(ways):
        _, flying[part] = send({way: own(way * reach, part)})
    for step in range(reach - 1, -1, -1):
        for part in range(2):
            got = {way: value.astype(jnp.float32) for way, value in flying[part].items()}
            if step:
                values = {way: got[way] + own(way * step, part) if way in got else own(way * step, part) for way in ways}
                values, flying[part] = send(values)
                flying[1 - part], _ = lax.optimization_barrier((flying[1 - part], values))
            else:
                flying[part] = own(0, part) + got[1] + got[-1]
    return jnp.concatenate(flying, axis=1)


def body(gradient, carried_error, q_start):
    gradient, carried_error = gradient[0].T, carried_error[0].T
    turned = group_sum(gradient, carried_error)
    summed = turned.T
    rank = q_start.shape[1]
    half_shape, share_shape, square = (HALF, rank), (SHARE + SLICE, rank), (rank, rank)
    send, keep = local_call(first_kernel, [half_shape] * 2, (q_start, summed))
    for iteration in range(ITERS):
        mine = keep + swap(send, "col", 1)
        mine = plane_sum(mine)
        other = swap(mine, "col", 1)
        last = iteration == ITERS - 1
        if last:
            flying = ring_step({1: mine, -1: mine})
        own, *others = local_call(
            column_kernel, [share_shape] * 4, (mine, other, turned),
            scratch=[(2 * HALF, rank), (QUAD * SHARE, rank), square],
        )
        share = quad_sum(own, others, "dp", 1)
        if last:
            (near, share) = lax.optimization_barrier((flying, share))
            flying = ring_step(near)
        share = share + swap(share, "dp", QUAD)
        if last:
            (middle, mine, share) = lax.optimization_barrier((flying, mine, share))
            flying = ring_step(middle)
            across = swap(mine, "dp", QUAD)
        shares = [share] + quad_steps([share] * 3, "dp", 1)
        if iteration < ITERS - 1:
            send, keep = local_call(
                middle_kernel, [half_shape] * 2, (*shares, summed),
                scratch=[square, q_start.shape, (rank, 2 * rank)],
            )
    far, across, shares = lax.optimization_barrier((flying, across, shares))
    blocks = [mine, near[-1], middle[-1], far[-1], across, far[1], middle[1], near[1]]
    all_mine = jnp.concatenate(blocks)
    all_other = jnp.concatenate([other] + [swap(block, "col", 1) for block in blocks[1:]])
    upper, q_factor = local_call(
        last_kernel, [square, q_start.shape], shares, scratch=[square, (rank, 2 * rank)], flops=FACTOR_FLOPS
    )
    new_error = apply_update(upper, q_factor, all_mine, all_other, gradient, carried_error)
    return (new_error.T[None], q_factor)


def solution(mesh):
    placed = (P("dp", None, "col"), P("dp", None, "col"), P("col", None))
    return jax.shard_map(
        body,
        mesh=mesh,
        in_specs=placed,
        out_specs=(P("dp", None, "col"), P("col", None)),
        check_vma=False,
    )
```
